32 devices in a mesh: grp: 2 (over x), attn: 8 (over z, y), ffn: 2 (over core).
Axes of the slice: x: 2, y: 2, z: 4, core: 2. Of those that a mesh axis runs over, the one named last changes fastest.
Arguments:
- queries: bfloat16 [64, 8192], P(('grp', 'attn', 'ffn')), parts along dimension 0, may hold values from -125 to 125
- key_cache: bfloat16 [64, 320, 1024], P(('grp', 'attn', 'ffn')), parts along dimension 0, may hold values from -6.1 to 6.1
- value_cache: bfloat16 [64, 320, 1024], P(('grp', 'attn', 'ffn')), parts along dimension 0, may hold values from -6 to 6
- lengths: int32 [64], P(('grp', 'attn', 'ffn')), parts along dimension 0, may hold values from 40 to 320, as said below
- slot_order: int32 [64], P('grp'), parts along dimension 0, may hold values from 0 to 31, each once
- kept_rows: int32 [64], P(('grp', 'ffn')), parts along dimension 0, may hold values 0 or 1
- residual: bfloat16 [64, 8192], P('grp', 'attn'), parts along dimension 0, may hold values from -6 to 6
- norm_gain: float32 [8192], P('attn'), may hold values from 0.1 to 1.9
- w_out: bfloat16 [8192, 8192], P(None, 'attn'), may hold values from -0.0625 to 0.0625
- w_gate: bfloat16 [8192, 16384], P(None, ('attn', 'ffn')), may hold values from -0.0625 to 0.0625
- w_up: bfloat16 [8192, 16384], P(None, ('attn', 'ffn')), may hold values from -0.0625 to 0.0625
- w_down: bfloat16 [16384, 8192], P(('attn', 'ffn')), may hold values from -0.0625 to 0.0625
Outputs:
- mixed: bfloat16 [64, 8192], P(('grp', 'ffn'), 'attn'), parts along dimension 0
The draws below stay inside these ranges and needn't reach their ends.
There are 2 independent parts, one for each index of `grp`. The reference program is written for one: setup_inputs(seed, part) draws one part's arguments, and reference() takes and returns one part's arrays. A program takes and returns all parts, laid end to end along the dimension named above; an argument that names none is the same for every part. Nothing has to cross between parts.
Inputs may be any that keep to these rules, and one draw needn't show every extreme that they name: `lengths`: every slot has at least 40 live entries and some slot has exactly 320.
All inputs are finite; a program needn't handle non-finite values. No bound on the sum of `kept_rows` on one device may be relied on, other than what follows from the above.
Results may differ from the reference program's by a relative error of at most 0.006.
Values may be sent and summed in bfloat16 or wider, within the bound.
A program may use at most 192 MiB of HBM per device.

```python
import jax
import jax.numpy as jnp
from jax import lax

D = 8192
QH = 64
KVH = 8
HD = 128
FFW = 16384
ROWS_DEV = 2
LMAX = 320
ROWS = 32


def shared_keys(key):
    return jnp.clip(jax.random.normal(key, (ROWS, LMAX, KVH * HD), jnp.float32), -6.0, 6.0)


def draw_key_cache(key, part):
    keys_base = shared_keys(key)
    return keys_base.astype(jnp.bfloat16)


def draw_queries(key, part):
    key = jax.random.fold_in(key, 5)
    return jnp.clip(jax.random.normal(key, (ROWS, D), jnp.float32), -6.0, 6.0).astype(jnp.bfloat16)


def draw_lengths(key, part):
    key = jax.random.fold_in(key, 7)
    k_one, k_two, k_three = jax.random.split(key, 3)
    floor_len = LMAX // 8
    block_top = jax.random.randint(k_one, (ROWS // ROWS_DEV,), LMAX // 4, LMAX + 1)
    spread_top = jnp.repeat(block_top, ROWS_DEV)
    raw_draw = jax.random.randint(k_two, (ROWS,), 0, 1 << 20)
    drawn_len = floor_len + raw_draw % (spread_top - floor_len + 1)
    chosen = jax.random.randint(k_three, (), 0, ROWS)
    return jnp.where(jnp.arange(ROWS) == chosen, LMAX, drawn_len).astype(jnp.int32)


def with_ends(entries, key, least, high):
    shape = entries.shape
    index_at = [jax.random.randint(jax.random.fold_in(key, axis), (), 0, shape[axis]) for axis in range(len(shape))]
    entries = entries.at[tuple(index_at)].set(least)
    longest = shape.index(max(shape))
    index_at[longest] = (index_at[longest] + 1) % shape[longest]
    return entries.at[tuple(index_at)].set(high)


def with_spikes(values, stream_key, source, target, shards_of, factor):
    def block_of(dim):
        return (jnp.arange(values.shape[dim]) // (values.shape[dim] // shards_of)).reshape((-1,) + (1,) * (values.ndim - 1 - dim))

    first = jax.random.permutation(stream_key, shards_of)[block_of(target)]
    far = (block_of(target) + shards_of // 2) % shards_of
    return jnp.where((block_of(source) == first) | (block_of(source) == far), factor * values, values)


def level_of(key, shape, pieces, least, top_value):
    gain, own = 1.0, jax.random.fold_in(key, 6)
    for dim, blocks in pieces:
        steps = jnp.exp(jax.random.uniform(jax.random.fold_in(own, dim), (blocks,), jnp.float32, least / len(pieces), top_value / len(pieces)))
        gain = gain * jnp.repeat(steps, shape[dim] // blocks).reshape([-1 if axis == dim else 1 for axis in range(len(shape))])
    return gain


def gaussian(rng, dims, width, limit, pieces=(), kind=jnp.bfloat16):
    result = jax.random.normal(rng, dims, jnp.float32) * width
    if len(pieces) > 0:
        result = level_of(rng, dims, pieces, -0.22, 0.18) * result
    return jnp.clip(result, min=-limit, max=limit).astype(kind)


def bell_draw_with(key, dims, spread, bound, cuts, heavy, held_as=jnp.bfloat16):
    drawn = spread * jax.random.normal(key, dims, jnp.float32)
    if cuts:
        drawn = drawn * level_of(key, dims, cuts, -0.22, 0.18)
    return jnp.clip(with_spikes(drawn, jax.random.fold_in(key, 3), *heavy), -bound, bound).astype(held_as)


def setup_inputs(seed: int = 0, part: int = 0) -> dict:
    streams_of = jax.random.split(jax.random.key(seed), 13)
    part_splits = jax.random.split(jax.random.fold_in(streams_of[12], part), 13)
    queries = draw_queries(jax.random.fold_in(jax.random.fold_in(streams_of[12], part), 71), part)
    key_cache = draw_key_cache(jax.random.fold_in(jax.random.fold_in(streams_of[12], part), 71), part)
    value_cache = gaussian(part_splits[2], (ROWS, LMAX, KVH * HD), 1.0, 6.0, ((0, 16),))
    lengths = draw_lengths(jax.random.fold_in(jax.random.fold_in(streams_of[12], part), 71), part)
    slot_order = jax.random.permutation(part_splits[4], ROWS).astype(jnp.int32)
    kept_rows = with_ends((jax.random.randint(part_splits[5], (ROWS,), 0, 4) < 3).astype(jnp.int32), jax.random.fold_in(part_splits[5], 1), 0, 1)
    residual = gaussian(part_splits[6], (ROWS, D), 0.5, 6.0, ((1, 8),))
    norm_gain = jnp.clip(1.0 + 0.18 * jax.random.normal(streams_of[7], (D,), jnp.float32), 0.1, 1.9)
    w_out = gaussian(streams_of[8], (D, D), D ** -0.5, 0.0625, ((1, 8),))
    w_gate = gaussian(streams_of[9], (D, FFW), D ** -0.5, 0.0625, ((1, 16),))
    w_up = gaussian(streams_of[10], (D, FFW), D ** -0.5, 0.0625, ((1, 16),))
    w_down = bell_draw_with(streams_of[11], (FFW, D), FFW ** -0.5, 0.0625, ((0, 16),), (0, 1, 16, 2.0))
    return dict(queries=queries, key_cache=key_cache, value_cache=value_cache, lengths=lengths, slot_order=slot_order, kept_rows=kept_rows, residual=residual, norm_gain=norm_gain, w_out=w_out, w_gate=w_gate, w_up=w_up, w_down=w_down)


NEG_BIG = -1e+30
EPSILON = 1e-05

def attend_row(inputs):
    query, key_rows, value_rows, length = inputs
    grouped = query.astype(jnp.float32).reshape(KVH, QH // KVH, HD)
    keys_full = key_rows.astype(jnp.float32).reshape(LMAX, KVH, HD)
    values_full = value_rows.astype(jnp.float32).reshape(LMAX, KVH, HD)
    scores = jnp.einsum('kgd,pkd->kgp', grouped, keys_full) * HD ** (-0.5)
    in_range = (jnp.arange(LMAX, dtype=jnp.int32) < length)[None, None, :]
    scores = jnp.where(in_range, scores, NEG_BIG)
    largest = lax.optimization_barrier(jnp.max(scores, axis=2))
    exponent = jnp.where(in_range, jnp.exp(scores - largest[..., None]), 0.0)
    totals = lax.optimization_barrier(jnp.sum(exponent, axis=2))
    rounded = lax.optimization_barrier(exponent.astype(jnp.bfloat16))
    weighted = jnp.einsum('kgp,pkd->kgd', rounded.astype(jnp.float32), values_full)
    return (weighted / totals[..., None]).reshape(D).astype(jnp.bfloat16)

def reference(queries, key_cache, value_cache, lengths, slot_order, kept_rows, residual, norm_gain, w_out, w_gate, w_up, w_down):
    context = lax.map(attend_row, (queries, key_cache, value_cache, lengths))
    attended = jnp.dot(context, w_out, preferred_element_type=jnp.float32)
    hidden = residual.astype(jnp.float32) + jnp.take(attended, slot_order, axis=0)
    mean_square = lax.optimization_barrier(jnp.mean(hidden * hidden, axis=1))
    normed = (hidden * lax.rsqrt(mean_square + EPSILON)[:, None] * norm_gain).astype(jnp.bfloat16)
    gate_sum = jnp.dot(normed, w_gate, preferred_element_type=jnp.float32)
    up_sum = jnp.dot(normed, w_up, preferred_element_type=jnp.float32)
    activated = (jax.nn.silu(gate_sum) * up_sum).astype(jnp.bfloat16)
    down = jnp.dot(activated, w_down, preferred_element_type=jnp.float32)
    return (hidden + kept_rows.astype(jnp.float32)[:, None] * down).astype(jnp.bfloat16)
```

```python
import jax
import jax.numpy as jnp
from jax import lax
from jax.experimental import pallas as pl
from jax.experimental.pallas import tpu as pltpu
from jax.sharding import PartitionSpec as P

D = 8192
QH = 64
KVH = 8
HD = 128


NEG_BIG = -1e30
EPSILON = 1e-05


def local_attention(queries, key_cache, value_cache, lengths):
    row_count = queries.shape[0]
    slot_count = key_cache.shape[1]
    grouped = queries.reshape(row_count, KVH, QH // KVH, HD)
    key_rows = key_cache.reshape(row_count, slot_count, KVH, HD)
    value_rows = value_cache.reshape(row_count, slot_count, KVH, HD)
    scores = jnp.einsum(
        "rkgd,rpkd->rkgp", grouped, key_rows, preferred_element_type=jnp.float32
    ) * HD ** (-0.5)
    in_range = (jnp.arange(slot_count, dtype=jnp.int32)[None, :] < lengths[:, None])[
        :, None, None, :
    ]
    scores = jnp.where(in_range, scores, NEG_BIG)
    largest = jnp.max(scores, axis=3)
    exponent = jnp.where(in_range, jnp.exp(scores - largest[..., None]), 0.0)
    totals = jnp.sum(exponent, axis=3)
    weighted = jnp.einsum(
        "rkgp,rpkd->rkgd",
        exponent.astype(jnp.bfloat16),
        value_rows,
        preferred_element_type=jnp.float32,
    )
    return (weighted / totals[..., None]).reshape(row_count, -1).astype(jnp.bfloat16)


def per_device(
    queries,
    key_cache,
    value_cache,
    lengths,
    slot_order,
    kept_rows,
    residual,
    norm_gain,
    w_out,
    w_gate,
    w_up,
    w_down,
):
    context = local_attention(queries, key_cache, value_cache, lengths)
    attended = jnp.dot(
        lax.all_gather(context, ("attn", "ffn"), axis=0, tiled=True),
        w_out,
        preferred_element_type=jnp.float32,
    )
    hidden = residual.astype(jnp.float32) + jnp.take(attended, slot_order, axis=0)
    squares = lax.psum(jnp.sum(hidden * hidden, axis=1), "attn")
    normed = (hidden * lax.rsqrt(squares / D + EPSILON)[:, None] * norm_gain).astype(jnp.bfloat16)
    all_rows = normed.shape[0]
    segment = lax.all_gather(normed, "attn", axis=1, tiled=True)
    gate_sum = jnp.dot(segment, w_gate, preferred_element_type=jnp.float32)
    up_sum = jnp.dot(segment, w_up, preferred_element_type=jnp.float32)
    activated = (jax.nn.silu(gate_sum) * up_sum).astype(jnp.bfloat16)
    partial_out = jnp.dot(activated, w_down, preferred_element_type=jnp.float32)
    share_rows = all_rows // lax.axis_size("ffn")
    summed = lax.psum_scatter(partial_out, "attn", scatter_dimension=1, tiled=True)
    summed = lax.psum_scatter(summed, "ffn", scatter_dimension=0, tiled=True)
    own_hidden = lax.dynamic_slice_in_dim(hidden, lax.axis_index("ffn") * share_rows, share_rows, 0)
    return (own_hidden + kept_rows.astype(jnp.float32)[:, None] * summed).astype(jnp.bfloat16)


MESH = pl.DeviceIdType.MESH
F32 = jnp.float32
BF16 = jnp.bfloat16
ZN = 4
NDEV = 16
ROWS = 32
HALF = 16
SPLIT = 512


def iota(shape, dim):
    return lax.broadcasted_iota(jnp.int32, shape, dim)


def fused_kernel(
    queries, keys, values, lengths, slot_order, kept_rows, residual, gain, w_out, w_gate, w_up, w_down,
    out,
    kbuf, vbuf, qbd, ctx, sel, pcx, pool, gbuf, ubuf, xbuf, acc_g, acc_u, hidden, hid_own, act,
    part, s1_send, s1_recv, s2_send, s2_recv, s3_send, s3_recv,
    kv_sem, pool_sem, down_sem, gate_sem, up_sem,
    ctx_send, ctx_recv, x_send, x_recv, hid_sem, s1_ssem, s1_rsem, s2_ssem, s2_rsem, s3_ssem, s3_rsem,
):
    attn = lax.axis_index("attn")
    c = lax.axis_index("ffn")
    z, y = attn // 2, attn % 2
    oz = lambda j: (z + j) % ZN
    block = lambda zz, yy, cc: (zz * 2 + yy) * 2 + cc
    core_id = {"attn": attn, "ffn": 1 - c}
    y_id = {"attn": z * 2 + 1 - y, "ffn": c}
    z_id = lambda j: {"attn": oz(j) * 2 + y, "ffn": c}

    def remote(src, dst, ssem, rsem, dev):
        return pltpu.make_async_remote_copy(
            src_ref=src, dst_ref=dst, send_sem=ssem, recv_sem=rsem, device_id=dev, device_id_type=MESH
        )

    barrier = pltpu.get_barrier_semaphore()
    for dev in (core_id, y_id, z_id(1), z_id(2), z_id(3)):
        pl.semaphore_signal(barrier, inc=1, device_id=dev, device_id_type=MESH)

    def kv_load(r):
        return (
            pltpu.make_async_copy(keys.at[r], kbuf.at[r], kv_sem.at[0, r]),
            pltpu.make_async_copy(values.at[r], vbuf.at[r], kv_sem.at[1, r]),
        )

    def out_load(k):
        return pltpu.make_async_copy(
            w_out.at[pl.ds(k * 1024, 1024), pl.ds(pl.multiple_of(c * SPLIT, SPLIT), SPLIT)],
            pool.at[k],
            pool_sem.at[k],
        )

    def step_block(s):
        kind, j = s // ZN, s % ZN
        yy = (y + kind % 2) % 2
        cc = (c + kind // 2) % 2
        return block(oz(j), yy, cc)

    def gate_load(s):
        b = step_block(s)
        rows = pl.ds(pl.multiple_of(b * SPLIT, SPLIT), SPLIT)
        return (
            pltpu.make_async_copy(w_gate.at[rows], gbuf.at[s], gate_sem.at[s]),
            pltpu.make_async_copy(w_up.at[rows], ubuf.at[s], up_sem.at[s]),
        )

    def down_load(i):
        q = i // 2
        t = oz(1 + q % ZN) * 2 + (y + 1 + q // ZN) % 2
        col = pl.multiple_of(t * 1024 + (i % 2) * SPLIT, SPLIT)
        slot = (i + 8) % 16
        return pltpu.make_async_copy(w_down.at[:, pl.ds(col, SPLIT)], pool.at[slot], down_sem.at[i])

    def start_loop(n, first, load):
        @pl.loop(first, n)
        def _(i):
            copies = load(i)
            for copy in copies if isinstance(copies, tuple) else (copies,):
                copy.start()

    for r in range(2):
        for copy in kv_load(r):
            copy.start()
    start_loop(8, 0, out_load)

    order = jnp.zeros((ROWS, 256), jnp.int32)
    sub = iota((ROWS, 256), 0)
    lane = iota((ROWS, 256), 1)
    for i in range(ROWS):
        order = jnp.where(sub == i, slot_order[i], order)
    for k in range(KVH):
        sel[k] = jnp.where(lane == order * 8 + k, 1.0, 0.0).astype(BF16)

    row8 = iota((8, HD), 0)
    for r in range(2):
        q_row = queries[...].astype(F32)[r : r + 1]
        for g in range(8):
            tiles = [
                jnp.where(
                    row8 == k,
                    jnp.broadcast_to(q_row[:, (k * 8 + g) * HD : (k * 8 + g + 1) * HD], (8, HD)),
                    0.0,
                )
                for k in range(KVH)
            ]
            qbd[r, pl.ds(g * 8, 8), :] = jnp.concatenate(tiles, axis=1)

    me = block(z, y, c)
    rows_out = []
    for r in range(2):
        for copy in kv_load(r):
            copy.wait()
        if r == 1:
            start_loop(NDEV, 0, gate_load)
        scores = lax.dot_general(
            qbd[r].astype(BF16), kbuf[r], (((1,), (1,)), ((), ())), preferred_element_type=F32
        ) * HD ** (-0.5)
        live = iota(scores.shape, 1) < lengths[r]
        scores = jnp.where(live, scores, NEG_BIG)
        largest = jnp.max(scores, axis=1, keepdims=True)
        exponent = jnp.where(live, jnp.exp(scores - largest), 0.0)
        totals = jnp.sum(exponent, axis=1, keepdims=True)
        weighted = jnp.dot(exponent.astype(BF16), vbuf[r], preferred_element_type=F32) / totals
        pieces = []
        for g in range(8):
            tile = jnp.zeros((8, HD), F32)
            for k in range(KVH):
                tile = jnp.where(row8 == k, weighted[g * 8 : (g + 1) * 8, k * HD : (k + 1) * HD], tile)
            pieces.append(tile)
        rows_out.append(jnp.concatenate(pieces, axis=1))
    ctx[me] = jnp.concatenate(rows_out, axis=0).astype(BF16)
    start_loop(8, 0, down_load)
    pl.semaphore_wait(barrier, 5)

    def gather_copies(buf, send, recv):
        def copy(b, k, dev):
            return remote(buf.at[b], buf.at[b], send.at[k], recv.at[b], dev)

        to_z = lambda j: copy(me, j - 1, z_id(j))
        to_y = lambda j: copy(block(oz(j), y, c), 3 + j, y_id)
        to_core = lambda kind, j: copy(block(oz(j), (y + kind) % 2, c), 7 + kind * ZN + j, core_id)

        def arrived(b):
            copy(b, 0, core_id).wait_recv()

        return to_z, to_y, to_core, arrived

    def gather(buf, send, recv, use):
        to_z, to_y, to_core, arrived = gather_copies(buf, send, recv)
        for j in (1, 3, 2):
            to_z(j).start()
        to_y(0).start()
        to_core(0, 0).start()
        use(0)

        @pl.loop(1, ZN)
        def _(j):
            arrived(block(oz(j), y, c))
            to_y(j).start()
            to_core(0, j).start()
            use(j)

        @pl.loop(0, ZN)
        def _(j):
            arrived(block(oz(j), 1 - y, c))
            to_core(1, j).start()
            use(ZN + j)

        @pl.loop(2 * ZN, 4 * ZN)
        def _(s):
            arrived(step_block(s))
            use(s)

    def gather_end(buf, send, recv):
        to_z, to_y, to_core, _ = gather_copies(buf, send, recv)
        for j in range(1, ZN):
            to_z(j).wait_send()
        for j in range(ZN):
            to_y(j).wait_send()
            to_core(0, j).wait_send()
            to_core(1, j).wait_send()

    gather(ctx, ctx_send, ctx_recv, lambda s: None)

    picked = jnp.dot(
        sel[...].reshape(256, 256), ctx[...].reshape(256, 1024), preferred_element_type=F32
    )
    pcx[...] = picked.astype(BF16).reshape(KVH, ROWS, 1024)

    attended = jnp.zeros((ROWS, SPLIT), F32)

    def out_step(k, total):
        out_load(k).wait()
        return total + jnp.dot(pcx[k], pool[k], preferred_element_type=F32)

    attended = lax.fori_loop(0, KVH, out_step, attended)
    mine = pl.ds(pl.multiple_of(c * SPLIT, SPLIT), SPLIT)
    hid = residual[:, mine].astype(F32) + attended
    square = jnp.sum(hid * hid, axis=1, keepdims=True)
    high = square.astype(BF16).astype(F32)
    mid = (square - high).astype(BF16).astype(F32)
    low = square - high - mid
    lane128 = iota((ROWS, 128), 1)
    tail = jnp.where(lane128 == 0, high, jnp.where(lane128 == 1, mid, jnp.where(lane128 == 2, low, 0.0)))
    xbuf[me, :, :SPLIT] = (hid * gain[:, mine]).astype(BF16)
    xbuf[me, :, SPLIT:] = tail.astype(BF16)
    hidden[...] = hid.reshape(2, HALF, SPLIT)
    acc_g[...] = jnp.zeros_like(acc_g)
    acc_u[...] = jnp.zeros_like(acc_u)

    @pl.loop(8, 16)
    def _(i):
        down_load(i).start()

    def gate_step(s):
        for copy in gate_load(s):
            copy.wait()
        x = xbuf[step_block(s), :, :SPLIT]
        acc_g[...] += jnp.dot(x, gbuf[s], preferred_element_type=F32)
        acc_u[...] += jnp.dot(x, ubuf[s], preferred_element_type=F32)

    gather(xbuf, x_send, x_recv, gate_step)

    hid_copy = remote(hidden.at[1 - c], hid_own.at[c], hid_sem.at[0], hid_sem.at[1], core_id)
    hid_copy.start()
    hid_own[c] = hidden[c]

    square = jnp.sum(jnp.sum(xbuf[:, :, SPLIT:].astype(F32), axis=0), axis=1, keepdims=True)
    scale = lax.rsqrt(square / D + EPSILON)
    gate = acc_g[...] * scale
    up = acc_u[...] * scale
    act[...] = (gate / (1.0 + jnp.exp(-gate)) * up).astype(BF16)

    def s1_copy(q):
        return remote(s1_send.at[q], s1_recv.at[q], s1_ssem.at[q], s1_rsem.at[q], core_id)

    def s2_copy(u):
        return remote(s2_send.at[u], s2_recv.at[u], s2_ssem.at[u], s2_rsem.at[u], y_id)

    def s3_copy(u):
        return remote(s3_send.at[u], s3_recv.at[u], s3_ssem.at[u], s3_rsem.at[u], z_id(1 + u))

    def down_step(q):
        for half in range(2):
            down_load(2 * q + half).wait()
            piece = jnp.dot(act[...], pool[(2 * q + half + 8) % 16], preferred_element_type=F32)
            part[q, :, :, half * SPLIT : (half + 1) * SPLIT] = piece.reshape(2, HALF, SPLIT)
        s1_send[q] = part[q, 1 - c].astype(BF16)
        s1_copy(q).start()

    def chip_sum(q):
        s1_copy(q).wait_recv()
        return part[q, c] + s1_recv[q].astype(F32)

    def pass_y(u):
        s2_send[u] = chip_sum(u).astype(BF16)
        s2_copy(u).start()

    def pair_sum(u):
        total = chip_sum(ZN + u)
        s2_copy(u).wait_recv()
        return total + s2_recv[u].astype(F32)

    down_step(0)

    @pl.loop(1, ZN)
    def _(q):
        down_step(q)
        pass_y(q - 1)

    down_step(ZN)
    pass_y(ZN - 1)

    @pl.loop(0, ZN - 1)
    def _(u):
        down_step(ZN + 1 + u)
        s3_send[u] = pair_sum(u).astype(BF16)
        s3_copy(u).start()

    total = pair_sum(ZN - 1)
    for u in range(ZN - 1):
        s3_copy(u).wait_recv()
        total = total + s3_recv[u].astype(F32)
    kept = jnp.zeros((HALF, 128), jnp.int32)
    sub16 = iota((HALF, 128), 0)
    for i in range(HALF):
        kept = jnp.where(sub16 == i, kept_rows[i], kept)
    kept = kept.astype(F32)[:, :1]
    hid_copy.wait()
    for half in range(2):
        cols = slice(half * SPLIT, (half + 1) * SPLIT)
        out[:, cols] = (hid_own[half] + kept * total[:, cols]).astype(BF16)

    gather_end(ctx, ctx_send, ctx_recv)
    gather_end(xbuf, x_send, x_recv)
    for q in range(8):
        s1_copy(q).wait_send()
    for u in range(ZN):
        s2_copy(u).wait_send()
    for u in range(ZN - 1):
        s3_copy(u).wait_send()


def fused_device(
    queries, key_cache, value_cache, lengths, slot_order, kept_rows, residual, norm_gain, w_out, w_gate, w_up, w_down
):
    vmem = pl.BlockSpec(memory_space=pltpu.VMEM)
    smem = pl.BlockSpec(memory_space=pltpu.SMEM)
    hbm = pl.BlockSpec(memory_space=pl.ANY)
    slots = key_cache.shape[1]
    dma = pltpu.SemaphoreType.DMA
    return pl.pallas_call(
        fused_kernel,
        out_shape=jax.ShapeDtypeStruct((HALF, 1024), BF16),
        in_specs=[vmem, hbm, hbm, smem, smem, smem, vmem, vmem, hbm, hbm, hbm, hbm],
        out_specs=vmem,
        scratch_shapes=[
            pltpu.VMEM((2, slots, 1024), BF16),
            pltpu.VMEM((2, slots, 1024), BF16),
            pltpu.VMEM((2, 64, 1024), F32),
            pltpu.VMEM((NDEV, 16, 1024), BF16),
            pltpu.VMEM((KVH, ROWS, 256), BF16),
            pltpu.VMEM((KVH, ROWS, 1024), BF16),
            pltpu.VMEM((16, 1024, SPLIT), BF16),
            pltpu.VMEM((NDEV, SPLIT, 1024), BF16),
            pltpu.VMEM((NDEV, SPLIT, 1024), BF16),
            pltpu.VMEM((NDEV, ROWS, SPLIT + 128), BF16),
            pltpu.VMEM((ROWS, 1024), F32),
            pltpu.VMEM((ROWS, 1024), F32),
            pltpu.VMEM((2, HALF, SPLIT), F32),
            pltpu.VMEM((2, HALF, SPLIT), F32),
            pltpu.VMEM((ROWS, 1024), BF16),
            pltpu.VMEM((8, 2, HALF, 1024), F32),
            pltpu.VMEM((8, HALF, 1024), BF16),
            pltpu.VMEM((8, HALF, 1024), BF16),
            pltpu.VMEM((4, HALF, 1024), BF16),
            pltpu.VMEM((4, HALF, 1024), BF16),
            pltpu.VMEM((3, HALF, 1024), BF16),
            pltpu.VMEM((3, HALF, 1024), BF16),
            dma((2, 2)), dma((8,)), dma((16,)), dma((16,)), dma((16,)),
            dma((15,)), dma((NDEV,)), dma((15,)), dma((NDEV,)), dma((2,)),
            dma((8,)), dma((8,)), dma((4,)), dma((4,)), dma((3,)), dma((3,)),
        ],
        compiler_params=pltpu.CompilerParams(
            collective_id=0, has_side_effects=True, vmem_limit_bytes=60 * 1024 * 1024
        ),
        cost_estimate=pl.CostEstimate(flops=2 * 32 * 29 * 1024 * 1024, bytes_accessed=60 * 1024 * 1024, transcendentals=0),
        name="decode_step",
    )(
        queries, key_cache, value_cache, lengths, slot_order, kept_rows, residual,
        norm_gain.reshape(1, -1), w_out, w_gate, w_up, w_down,
    )


def solution(mesh):
    return jax.shard_map(
        fused_device if mesh.shape["attn"] == 8 and mesh.shape["ffn"] == 2 else per_device,
        mesh=mesh,
        in_specs=(
            P(("grp", "attn", "ffn"), None),
            P(("grp", "attn", "ffn"), None, None),
            P(("grp", "attn", "ffn"), None, None),
            P(("grp", "attn", "ffn")),
            P("grp"),
            P(("grp", "ffn")),
            P("grp", "attn"),
            P("attn"),
            P(None, "attn"),
            P(None, ("attn", "ffn")),
            P(None, ("attn", "ffn")),
            P(("attn", "ffn"), None),
        ),
        out_specs=P(("grp", "ffn"), "attn"),
        check_vma=False,
    )
```

```python
import jax
import jax.numpy as jnp
from jax import lax
from jax.experimental import pallas as pl
from jax.experimental.pallas import tpu as pltpu
from jax.sharding import PartitionSpec as P

D = 8192
QH = 64
KVH = 8
HD = 128


NEG_BIG = -1e30
EPSILON = 1e-05


def local_attention(queries, key_cache, value_cache, lengths):
    row_count = queries.shape[0]
    slot_count = key_cache.shape[1]
    grouped = queries.reshape(row_count, KVH, QH // KVH, HD)
    key_rows = key_cache.reshape(row_count, slot_count, KVH, HD)
    value_rows = value_cache.reshape(row_count, slot_count, KVH, HD)
    scores = jnp.einsum(
        "rkgd,rpkd->rkgp", grouped, key_rows, preferred_element_type=jnp.float32
    ) * HD ** (-0.5)
    in_range = (jnp.arange(slot_count, dtype=jnp.int32)[None, :] < lengths[:, None])[
        :, None, None, :
    ]
    scores = jnp.where(in_range, scores, NEG_BIG)
    largest = jnp.max(scores, axis=3)
    exponent = jnp.where(in_range, jnp.exp(scores - largest[..., None]), 0.0)
    totals = jnp.sum(exponent, axis=3)
    weighted = jnp.einsum(
        "rkgp,rpkd->rkgd",
        exponent.astype(jnp.bfloat16),
        value_rows,
        preferred_element_type=jnp.float32,
    )
    return (weighted / totals[..., None]).reshape(row_count, -1).astype(jnp.bfloat16)


def per_device(
    queries,
    key_cache,
    value_cache,
    lengths,
    slot_order,
    kept_rows,
    residual,
    norm_gain,
    w_out,
    w_gate,
    w_up,
    w_down,
):
    context = local_attention(queries, key_cache, value_cache, lengths)
    attended = jnp.dot(
        lax.all_gather(context, ("attn", "ffn"), axis=0, tiled=True),
        w_out,
        preferred_element_type=jnp.float32,
    )
    hidden = residual.astype(jnp.float32) + jnp.take(attended, slot_order, axis=0)
    squares = lax.psum(jnp.sum(hidden * hidden, axis=1), "attn")
    normed = (hidden * lax.rsqrt(squares / D + EPSILON)[:, None] * norm_gain).astype(jnp.bfloat16)
    all_rows = normed.shape[0]
    segment = lax.all_gather(normed, "attn", axis=1, tiled=True)
    gate_sum = jnp.dot(segment, w_gate, preferred_element_type=jnp.float32)
    up_sum = jnp.dot(segment, w_up, preferred_element_type=jnp.float32)
    activated = (jax.nn.silu(gate_sum) * up_sum).astype(jnp.bfloat16)
    partial_out = jnp.dot(activated, w_down, preferred_element_type=jnp.float32)
    share_rows = all_rows // lax.axis_size("ffn")
    summed = lax.psum_scatter(partial_out, "attn", scatter_dimension=1, tiled=True)
    summed = lax.psum_scatter(summed, "ffn", scatter_dimension=0, tiled=True)
    own_hidden = lax.dynamic_slice_in_dim(hidden, lax.axis_index("ffn") * share_rows, share_rows, 0)
    return (own_hidden + kept_rows.astype(jnp.float32)[:, None] * summed).astype(jnp.bfloat16)


MESH = pl.DeviceIdType.MESH
F32 = jnp.float32
BF16 = jnp.bfloat16
ZN = 4
NDEV = 16
ROWS = 32
HALF = 16
SPLIT = 512


def iota(shape, dim):
    return lax.broadcasted_iota(jnp.int32, shape, dim)


def fused_kernel(
    queries, keys, values, lengths, slot_order, kept_rows, residual, gain, w_out, w_gate, w_up, w_down,
    out,
    kbuf, vbuf, qbd, ctx, sel, pcx, pool, gbuf, ubuf, xbuf, acc_g, acc_u, hidden, hid_own, act,
    part, s1_send, s1_recv, s2_send, s2_recv, s3_send, s3_recv,
    kv_sem, pool_sem, down_sem, gate_sem, up_sem,
    ctx_send, ctx_recv, x_send, x_recv, hid_sem, s1_ssem, s1_rsem, s2_ssem, s2_rsem, s3_ssem, s3_rsem,
):
    attn = lax.axis_index("attn")
    c = lax.axis_index("ffn")
    z, y = attn // 2, attn % 2
    oz = lambda j: (z + j) % ZN
    block = lambda zz, yy, cc: (zz * 2 + yy) * 2 + cc
    core_id = {"attn": attn, "ffn": 1 - c}
    y_id = {"attn": z * 2 + 1 - y, "ffn": c}
    z_id = lambda j: {"attn": oz(j) * 2 + y, "ffn": c}

    def remote(src, dst, ssem, rsem, dev):
        return pltpu.make_async_remote_copy(
            src_ref=src, dst_ref=dst, send_sem=ssem, recv_sem=rsem, device_id=dev, device_id_type=MESH
        )

    barrier = pltpu.get_barrier_semaphore()
    for dev in (core_id, y_id, z_id(1), z_id(2), z_id(3)):
        pl.semaphore_signal(barrier, inc=1, device_id=dev, device_id_type=MESH)

    def kv_load(r):
        return (
            pltpu.make_async_copy(keys.at[r], kbuf.at[r], kv_sem.at[0, r]),
            pltpu.make_async_copy(values.at[r], vbuf.at[r], kv_sem.at[1, r]),
        )

    def out_load(k):
        return pltpu.make_async_copy(
            w_out.at[pl.ds(k * 1024, 1024), pl.ds(pl.multiple_of(c * SPLIT, SPLIT), SPLIT)],
            pool.at[k],
            pool_sem.at[k],
        )

    def step_block(s):
        kind, j = s // ZN, s % ZN
        yy = (y + kind % 2) % 2
        cc = (c + kind // 2) % 2
        return block(oz(j), yy, cc)

    def gate_load(s):
        b = step_block(s)
        rows = pl.ds(pl.multiple_of(b * SPLIT, SPLIT), SPLIT)
        return (
            pltpu.make_async_copy(w_gate.at[rows], gbuf.at[s], gate_sem.at[s]),
            pltpu.make_async_copy(w_up.at[rows], ubuf.at[s], up_sem.at[s]),
        )

    def down_load(i):
        q = i // 2
        t = oz(1 + q % ZN) * 2 + (y + 1 + q // ZN) % 2
        col = pl.multiple_of(t * 1024 + (i % 2) * SPLIT, SPLIT)
        slot = (i + 8) % 16
        return pltpu.make_async_copy(w_down.at[:, pl.ds(col, SPLIT)], pool.at[slot], down_sem.at[i])

    def start_loop(n, first, load):
        @pl.loop(first, n)
        def _(i):
            copies = load(i)
            for copy in copies if isinstance(copies, tuple) else (copies,):
                copy.start(priority=1)

    for r in range(2):
        for copy in kv_load(r):
            copy.start()
    start_loop(8, 0, out_load)

    order = jnp.zeros((ROWS, 256), jnp.int32)
    sub = iota((ROWS, 256), 0)
    lane = iota((ROWS, 256), 1)
    for i in range(ROWS):
        order = jnp.where(sub == i, slot_order[i], order)
    for k in range(KVH):
        sel[k] = jnp.where(lane == order * 8 + k, 1.0, 0.0).astype(BF16)

    row8 = iota((8, HD), 0)
    for r in range(2):
        q_row = queries[...].astype(F32)[r : r + 1]
        for g in range(8):
            tiles = [
                jnp.where(
                    row8 == k,
                    jnp.broadcast_to(q_row[:, (k * 8 + g) * HD : (k * 8 + g + 1) * HD], (8, HD)),
                    0.0,
                )
                for k in range(KVH)
            ]
            qbd[r, pl.ds(g * 8, 8), :] = jnp.concatenate(tiles, axis=1)

    me = block(z, y, c)
    rows_out = []
    for r in range(2):
        for copy in kv_load(r):
            copy.wait()
        if r == 1:
            start_loop(NDEV, 0, gate_load)
        scores = lax.dot_general(
            qbd[r].astype(BF16), kbuf[r], (((1,), (1,)), ((), ())), preferred_element_type=F32
        ) * HD ** (-0.5)
        live = iota(scores.shape, 1) < lengths[r]
        scores = jnp.where(live, scores, NEG_BIG)
        largest = jnp.max(scores, axis=1, keepdims=True)
        exponent = jnp.where(live, jnp.exp(scores - largest), 0.0)
        totals = jnp.sum(exponent, axis=1, keepdims=True)
        weighted = jnp.dot(exponent.astype(BF16), vbuf[r], preferred_element_type=F32) / totals
        pieces = []
        for g in range(8):
            tile = jnp.zeros((8, HD), F32)
            for k in range(KVH):
                tile = jnp.where(row8 == k, weighted[g * 8 : (g + 1) * 8, k * HD : (k + 1) * HD], tile)
            pieces.append(tile)
        rows_out.append(jnp.concatenate(pieces, axis=1))
    ctx[me] = jnp.concatenate(rows_out, axis=0).astype(BF16)
    start_loop(8, 0, down_load)
    pl.semaphore_wait(barrier, 5)

    def gather_copies(buf, send, recv):
        def copy(b, k, dev):
            return remote(buf.at[b], buf.at[b], send.at[k], recv.at[b], dev)

        to_z = lambda j: copy(me, j - 1, z_id(j))
        to_y = lambda j: copy(block(oz(j), y, c), 3 + j, y_id)
        to_core = lambda kind, j: copy(block(oz(j), (y + kind) % 2, c), 7 + kind * ZN + j, core_id)

        def arrived(b):
            copy(b, 0, core_id).wait_recv()

        return to_z, to_y, to_core, arrived

    def gather(buf, send, recv, use):
        to_z, to_y, to_core, arrived = gather_copies(buf, send, recv)
        for j in (1, 3, 2):
            to_z(j).start()
        to_y(0).start()
        to_core(0, 0).start()
        use(0)

        @pl.loop(1, ZN)
        def _(j):
            arrived(block(oz(j), y, c))
            to_y(j).start()
            to_core(0, j).start()
            use(j)

        @pl.loop(0, ZN)
        def _(j):
            arrived(block(oz(j), 1 - y, c))
            to_core(1, j).start()
            use(ZN + j)

        @pl.loop(2 * ZN, 4 * ZN)
        def _(s):
            arrived(step_block(s))
            use(s)

    def gather_end(buf, send, recv):
        to_z, to_y, to_core, _ = gather_copies(buf, send, recv)
        for j in range(1, ZN):
            to_z(j).wait_send()
        for j in range(ZN):
            to_y(j).wait_send()
            to_core(0, j).wait_send()
            to_core(1, j).wait_send()

    gather(ctx, ctx_send, ctx_recv, lambda s: None)

    picked = jnp.dot(
        sel[...].reshape(256, 256), ctx[...].reshape(256, 1024), preferred_element_type=F32
    )
    pcx[...] = picked.astype(BF16).reshape(KVH, ROWS, 1024)

    attended = jnp.zeros((ROWS, SPLIT), F32)

    def out_step(k, total):
        out_load(k).wait()
        return total + jnp.dot(pcx[k], pool[k], preferred_element_type=F32)

    attended = lax.fori_loop(0, KVH, out_step, attended)
    mine = pl.ds(pl.multiple_of(c * SPLIT, SPLIT), SPLIT)
    hid = residual[:, mine].astype(F32) + attended
    square = jnp.sum(hid * hid, axis=1, keepdims=True)
    high = square.astype(BF16).astype(F32)
    mid = (square - high).astype(BF16).astype(F32)
    low = square - high - mid
    lane128 = iota((ROWS, 128), 1)
    tail = jnp.where(lane128 == 0, high, jnp.where(lane128 == 1, mid, jnp.where(lane128 == 2, low, 0.0)))
    xbuf[me, :, :SPLIT] = (hid * gain[:, mine]).astype(BF16)
    xbuf[me, :, SPLIT:] = tail.astype(BF16)
    hidden[...] = hid.reshape(2, HALF, SPLIT)
    acc_g[...] = jnp.zeros_like(acc_g)
    acc_u[...] = jnp.zeros_like(acc_u)

    @pl.loop(8, 16)
    def _(i):
        down_load(i).start(priority=1)

    def gate_step(s):
        for copy in gate_load(s):
            copy.wait()
        x = xbuf[step_block(s), :, :SPLIT]
        acc_g[...] += jnp.dot(x, gbuf[s], preferred_element_type=F32)
        acc_u[...] += jnp.dot(x, ubuf[s], preferred_element_type=F32)

    gather(xbuf, x_send, x_recv, gate_step)

    hid_copy = remote(hidden.at[1 - c], hid_own.at[c], hid_sem.at[0], hid_sem.at[1], core_id)
    hid_copy.start()
    hid_own[c] = hidden[c]

    square = jnp.sum(jnp.sum(xbuf[:, :, SPLIT:].astype(F32), axis=0), axis=1, keepdims=True)
    scale = lax.rsqrt(square / D + EPSILON)
    gate = acc_g[...] * scale
    up = acc_u[...] * scale
    act[...] = (gate / (1.0 + jnp.exp(-gate)) * up).astype(BF16)

    def s1_copy(q):
        return remote(s1_send.at[q], s1_recv.at[q], s1_ssem.at[q], s1_rsem.at[q], core_id)

    def s2_copy(u):
        return remote(s2_send.at[u], s2_recv.at[u], s2_ssem.at[u], s2_rsem.at[u], y_id)

    def s3_copy(u):
        return remote(s3_send.at[u], s3_recv.at[u], s3_ssem.at[u], s3_rsem.at[u], z_id(1 + u))

    def down_step(q):
        for half in range(2):
            down_load(2 * q + half).wait()
            piece = jnp.dot(act[...], pool[(2 * q + half + 8) % 16], preferred_element_type=F32)
            part[q, :, :, half * SPLIT : (half + 1) * SPLIT] = piece.reshape(2, HALF, SPLIT)
        s1_send[q] = part[q, 1 - c].astype(BF16)
        s1_copy(q).start()

    def chip_sum(q):
        s1_copy(q).wait_recv()
        return part[q, c] + s1_recv[q].astype(F32)

    def pass_y(u):
        s2_send[u] = chip_sum(u).astype(BF16)
        s2_copy(u).start()

    def pair_sum(u):
        total = chip_sum(ZN + u)
        s2_copy(u).wait_recv()
        return total + s2_recv[u].astype(F32)

    down_step(0)

    @pl.loop(1, ZN)
    def _(q):
        down_step(q)
        pass_y(q - 1)

    down_step(ZN)
    pass_y(ZN - 1)

    @pl.loop(0, ZN - 1)
    def _(u):
        down_step(ZN + 1 + u)
        s3_send[u] = pair_sum(u).astype(BF16)
        s3_copy(u).start()

    total = pair_sum(ZN - 1)
    for u in range(ZN - 1):
        s3_copy(u).wait_recv()
        total = total + s3_recv[u].astype(F32)
    kept = jnp.zeros((HALF, 128), jnp.int32)
    sub16 = iota((HALF, 128), 0)
    for i in range(HALF):
        kept = jnp.where(sub16 == i, kept_rows[i], kept)
    kept = kept.astype(F32)[:, :1]
    hid_copy.wait()
    for half in range(2):
        cols = slice(half * SPLIT, (half + 1) * SPLIT)
        out[:, cols] = (hid_own[half] + kept * total[:, cols]).astype(BF16)

    gather_end(ctx, ctx_send, ctx_recv)
    gather_end(xbuf, x_send, x_recv)
    for q in range(8):
        s1_copy(q).wait_send()
    for u in range(ZN):
        s2_copy(u).wait_send()
    for u in range(ZN - 1):
        s3_copy(u).wait_send()


def fused_device(
    queries, key_cache, value_cache, lengths, slot_order, kept_rows, residual, norm_gain, w_out, w_gate, w_up, w_down
):
    vmem = pl.BlockSpec(memory_space=pltpu.VMEM)
    smem = pl.BlockSpec(memory_space=pltpu.SMEM)
    hbm = pl.BlockSpec(memory_space=pl.ANY)
    slots = key_cache.shape[1]
    dma = pltpu.SemaphoreType.DMA
    return pl.pallas_call(
        fused_kernel,
        out_shape=jax.ShapeDtypeStruct((HALF, 1024), BF16),
        in_specs=[vmem, hbm, hbm, smem, smem, smem, vmem, vmem, hbm, hbm, hbm, hbm],
        out_specs=vmem,
        scratch_shapes=[
            pltpu.VMEM((2, slots, 1024), BF16),
            pltpu.VMEM((2, slots, 1024), BF16),
            pltpu.VMEM((2, 64, 1024), F32),
            pltpu.VMEM((NDEV, 16, 1024), BF16),
            pltpu.VMEM((KVH, ROWS, 256), BF16),
            pltpu.VMEM((KVH, ROWS, 1024), BF16),
            pltpu.VMEM((16, 1024, SPLIT), BF16),
            pltpu.VMEM((NDEV, SPLIT, 1024), BF16),
            pltpu.VMEM((NDEV, SPLIT, 1024), BF16),
            pltpu.VMEM((NDEV, ROWS, SPLIT + 128), BF16),
            pltpu.VMEM((ROWS, 1024), F32),
            pltpu.VMEM((ROWS, 1024), F32),
            pltpu.VMEM((2, HALF, SPLIT), F32),
            pltpu.VMEM((2, HALF, SPLIT), F32),
            pltpu.VMEM((ROWS, 1024), BF16),
            pltpu.VMEM((8, 2, HALF, 1024), F32),
            pltpu.VMEM((8, HALF, 1024), BF16),
            pltpu.VMEM((8, HALF, 1024), BF16),
            pltpu.VMEM((4, HALF, 1024), BF16),
            pltpu.VMEM((4, HALF, 1024), BF16),
            pltpu.VMEM((3, HALF, 1024), BF16),
            pltpu.VMEM((3, HALF, 1024), BF16),
            dma((2, 2)), dma((8,)), dma((16,)), dma((16,)), dma((16,)),
            dma((15,)), dma((NDEV,)), dma((15,)), dma((NDEV,)), dma((2,)),
            dma((8,)), dma((8,)), dma((4,)), dma((4,)), dma((3,)), dma((3,)),
        ],
        compiler_params=pltpu.CompilerParams(
            collective_id=0, has_side_effects=True, vmem_limit_bytes=60 * 1024 * 1024
        ),
        cost_estimate=pl.CostEstimate(flops=2 * 32 * 29 * 1024 * 1024, bytes_accessed=60 * 1024 * 1024, transcendentals=0),
        name="decode_step",
    )(
        queries, key_cache, value_cache, lengths, slot_order, kept_rows, residual,
        norm_gain.reshape(1, -1), w_out, w_gate, w_up, w_down,
    )


def solution(mesh):
    return jax.shard_map(
        fused_device if mesh.shape["attn"] == 8 and mesh.shape["ffn"] == 2 else per_device,
        mesh=mesh,
        in_specs=(
            P(("grp", "attn", "ffn"), None),
            P(("grp", "attn", "ffn"), None, None),
            P(("grp", "attn", "ffn"), None, None),
            P(("grp", "attn", "ffn")),
            P("grp"),
            P(("grp", "ffn")),
            P("grp", "attn"),
            P("attn"),
            P(None, "attn"),
            P(None, ("attn", "ffn")),
            P(None, ("attn", "ffn")),
            P(("attn", "ffn"), None),
        ),
        out_specs=P(("grp", "ffn"), "attn"),
        check_vma=False,
    )
```

```python
import jax
import jax.numpy as jnp
from jax import lax
from jax.experimental import pallas as pl
from jax.experimental.pallas import tpu as pltpu
from jax.sharding import PartitionSpec as P

D = 8192
QH = 64
KVH = 8
HD = 128


NEG_BIG = -1e30
EPSILON = 1e-05


def local_attention(queries, key_cache, value_cache, lengths):
    row_count = queries.shape[0]
    slot_count = key_cache.shape[1]
    grouped = queries.reshape(row_count, KVH, QH // KVH, HD)
    key_rows = key_cache.reshape(row_count, slot_count, KVH, HD)
    value_rows = value_cache.reshape(row_count, slot_count, KVH, HD)
    scores = jnp.einsum(
        "rkgd,rpkd->rkgp", grouped, key_rows, preferred_element_type=jnp.float32
    ) * HD ** (-0.5)
    in_range = (jnp.arange(slot_count, dtype=jnp.int32)[None, :] < lengths[:, None])[
        :, None, None, :
    ]
    scores = jnp.where(in_range, scores, NEG_BIG)
    largest = jnp.max(scores, axis=3)
    exponent = jnp.where(in_range, jnp.exp(scores - largest[..., None]), 0.0)
    totals = jnp.sum(exponent, axis=3)
    weighted = jnp.einsum(
        "rkgp,rpkd->rkgd",
        exponent.astype(jnp.bfloat16),
        value_rows,
        preferred_element_type=jnp.float32,
    )
    return (weighted / totals[..., None]).reshape(row_count, -1).astype(jnp.bfloat16)


def per_device(
    queries,
    key_cache,
    value_cache,
    lengths,
    slot_order,
    kept_rows,
    residual,
    norm_gain,
    w_out,
    w_gate,
    w_up,
    w_down,
):
    context = local_attention(queries, key_cache, value_cache, lengths)
    attended = jnp.dot(
        lax.all_gather(context, ("attn", "ffn"), axis=0, tiled=True),
        w_out,
        preferred_element_type=jnp.float32,
    )
    hidden = residual.astype(jnp.float32) + jnp.take(attended, slot_order, axis=0)
    squares = lax.psum(jnp.sum(hidden * hidden, axis=1), "attn")
    normed = (hidden * lax.rsqrt(squares / D + EPSILON)[:, None] * norm_gain).astype(jnp.bfloat16)
    all_rows = normed.shape[0]
    segment = lax.all_gather(normed, "attn", axis=1, tiled=True)
    gate_sum = jnp.dot(segment, w_gate, preferred_element_type=jnp.float32)
    up_sum = jnp.dot(segment, w_up, preferred_element_type=jnp.float32)
    activated = (jax.nn.silu(gate_sum) * up_sum).astype(jnp.bfloat16)
    partial_out = jnp.dot(activated, w_down, preferred_element_type=jnp.float32)
    share_rows = all_rows // lax.axis_size("ffn")
    summed = lax.psum_scatter(partial_out, "attn", scatter_dimension=1, tiled=True)
    summed = lax.psum_scatter(summed, "ffn", scatter_dimension=0, tiled=True)
    own_hidden = lax.dynamic_slice_in_dim(hidden, lax.axis_index("ffn") * share_rows, share_rows, 0)
    return (own_hidden + kept_rows.astype(jnp.float32)[:, None] * summed).astype(jnp.bfloat16)


MESH = pl.DeviceIdType.MESH
F32 = jnp.float32
BF16 = jnp.bfloat16
ZN = 4
NDEV = 16
ROWS = 32
HALF = 16
SPLIT = 512


def iota(shape, dim):
    return lax.broadcasted_iota(jnp.int32, shape, dim)


def fused_kernel(
    queries, keys, values, lengths, slot_order, kept_rows, residual, gain, w_out, w_gate, w_up, w_down,
    out,
    kbuf, vbuf, qbd, ctx, sel, pcx, pool, gbuf, ubuf, xbuf, acc_g, acc_u, hidden, hid_own, act,
    part, s1_send, s1_recv, s2_send, s2_recv, s3_send, s3_recv,
    kv_sem, pool_sem, down_sem, gate_sem, up_sem,
    ctx_send, ctx_recv, x_send, x_recv, hid_sem, s1_ssem, s1_rsem, s2_ssem, s2_rsem, s3_ssem, s3_rsem,
):
    attn = lax.axis_index("attn")
    c = lax.axis_index("ffn")
    z, y = attn // 2, attn % 2
    oz = lambda j: (z // 2 + j // 2) % 2 * 2 + (z % 2 + j % 2) % 2
    block = lambda zz, yy, cc: (zz * 2 + yy) * 2 + cc
    core_id = {"attn": attn, "ffn": 1 - c}
    y_id = {"attn": z * 2 + 1 - y, "ffn": c}
    z_id = lambda j: {"attn": oz(j) * 2 + y, "ffn": c}

    def remote(src, dst, ssem, rsem, dev):
        return pltpu.make_async_remote_copy(
            src_ref=src, dst_ref=dst, send_sem=ssem, recv_sem=rsem, device_id=dev, device_id_type=MESH
        )

    barrier = pltpu.get_barrier_semaphore()
    for dev in (core_id, y_id, z_id(1), z_id(2), z_id(3)):
        pl.semaphore_signal(barrier, inc=1, device_id=dev, device_id_type=MESH)

    def kv_load(r):
        return (
            pltpu.make_async_copy(keys.at[r], kbuf.at[r], kv_sem.at[0, r]),
            pltpu.make_async_copy(values.at[r], vbuf.at[r], kv_sem.at[1, r]),
        )

    def out_load(k):
        return pltpu.make_async_copy(
            w_out.at[pl.ds(k * 1024, 1024), pl.ds(pl.multiple_of(c * SPLIT, SPLIT), SPLIT)],
            pool.at[k],
            pool_sem.at[k],
        )

    def step_block(s):
        kind, j = s // ZN, s % ZN
        yy = (y + kind % 2) % 2
        cc = (c + kind // 2) % 2
        return block(oz(j), yy, cc)

    def gate_load(s):
        b = step_block(s)
        rows = pl.ds(pl.multiple_of(b * SPLIT, SPLIT), SPLIT)
        return (
            pltpu.make_async_copy(w_gate.at[rows], gbuf.at[s], gate_sem.at[s]),
            pltpu.make_async_copy(w_up.at[rows], ubuf.at[s], up_sem.at[s]),
        )

    def down_load(i):
        q = i // 2
        t = oz(1 + q % ZN) * 2 + (y + 1 + q // ZN) % 2
        col = pl.multiple_of(t * 1024 + (i % 2) * SPLIT, SPLIT)
        slot = (i + 8) % 16
        return pltpu.make_async_copy(w_down.at[:, pl.ds(col, SPLIT)], pool.at[slot], down_sem.at[i])

    def start_loop(n, first, load):
        @pl.loop(first, n)
        def _(i):
            copies = load(i)
            for copy in copies if isinstance(copies, tuple) else (copies,):
                copy.start(priority=1)

    for r in range(2):
        for copy in kv_load(r):
            copy.start()
    start_loop(8, 0, out_load)

    order = jnp.zeros((ROWS, 256), jnp.int32)
    sub = iota((ROWS, 256), 0)
    lane = iota((ROWS, 256), 1)
    for i in range(ROWS):
        order = jnp.where(sub == i, slot_order[i], order)
    for k in range(KVH):
        sel[k] = jnp.where(lane == order * 8 + k, 1.0, 0.0).astype(BF16)

    row8 = iota((8, HD), 0)
    for r in range(2):
        q_row = queries[...].astype(F32)[r : r + 1]
        for g in range(8):
            tiles = [
                jnp.where(
                    row8 == k,
                    jnp.broadcast_to(q_row[:, (k * 8 + g) * HD : (k * 8 + g + 1) * HD], (8, HD)),
                    0.0,
                )
                for k in range(KVH)
            ]
            qbd[r, pl.ds(g * 8, 8), :] = jnp.concatenate(tiles, axis=1)

    me = block(z, y, c)
    rows_out = []
    for r in range(2):
        for copy in kv_load(r):
            copy.wait()
        if r == 1:
            start_loop(NDEV, 0, gate_load)
        scores = lax.dot_general(
            qbd[r].astype(BF16), kbuf[r], (((1,), (1,)), ((), ())), preferred_element_type=F32
        ) * HD ** (-0.5)
        live = iota(scores.shape, 1) < lengths[r]
        scores = jnp.where(live, scores, NEG_BIG)
        largest = jnp.max(scores, axis=1, keepdims=True)
        exponent = jnp.where(live, jnp.exp(scores - largest), 0.0)
        totals = jnp.sum(exponent, axis=1, keepdims=True)
        weighted = jnp.dot(exponent.astype(BF16), vbuf[r], preferred_element_type=F32) / totals
        pieces = []
        for g in range(8):
            tile = jnp.zeros((8, HD), F32)
            for k in range(KVH):
                tile = jnp.where(row8 == k, weighted[g * 8 : (g + 1) * 8, k * HD : (k + 1) * HD], tile)
            pieces.append(tile)
        rows_out.append(jnp.concatenate(pieces, axis=1))
    ctx[me] = jnp.concatenate(rows_out, axis=0).astype(BF16)
    start_loop(8, 0, down_load)
    pl.semaphore_wait(barrier, 5)

    def gather_copies(buf, send, recv):
        def copy(b, k, dev):
            return remote(buf.at[b], buf.at[b], send.at[k], recv.at[b], dev)

        to_z = lambda j: copy(me, j - 1, z_id(j))
        to_y = lambda j: copy(block(oz(j), y, c), 3 + j, y_id)
        to_core = lambda kind, j: copy(block(oz(j), (y + kind) % 2, c), 7 + kind * ZN + j, core_id)

        def arrived(b):
            copy(b, 0, core_id).wait_recv()

        return to_z, to_y, to_core, arrived

    def gather(buf, send, recv, use):
        to_z, to_y, to_core, arrived = gather_copies(buf, send, recv)
        for j in (1, 3, 2):
            to_z(j).start()
        to_y(0).start()
        to_core(0, 0).start()
        use(0)

        @pl.loop(1, ZN)
        def _(j):
            arrived(block(oz(j), y, c))
            to_y(j).start()
            to_core(0, j).start()
            use(j)

        @pl.loop(0, ZN)
        def _(j):
            arrived(block(oz(j), 1 - y, c))
            to_core(1, j).start()
            use(ZN + j)

        @pl.loop(2 * ZN, 4 * ZN)
        def _(s):
            arrived(step_block(s))
            use(s)

    def gather_end(buf, send, recv):
        to_z, to_y, to_core, _ = gather_copies(buf, send, recv)
        for j in range(1, ZN):
            to_z(j).wait_send()
        for j in range(ZN):
            to_y(j).wait_send()
            to_core(0, j).wait_send()
            to_core(1, j).wait_send()

    gather(ctx, ctx_send, ctx_recv, lambda s: None)

    picked = jnp.dot(
        sel[...].reshape(256, 256), ctx[...].reshape(256, 1024), preferred_element_type=F32
    )
    pcx[...] = picked.astype(BF16).reshape(KVH, ROWS, 1024)

    attended = jnp.zeros((ROWS, SPLIT), F32)

    def out_step(k, total):
        out_load(k).wait()
        return total + jnp.dot(pcx[k], pool[k], preferred_element_type=F32)

    attended = lax.fori_loop(0, KVH, out_step, attended)
    mine = pl.ds(pl.multiple_of(c * SPLIT, SPLIT), SPLIT)
    hid = residual[:, mine].astype(F32) + attended
    square = jnp.sum(hid * hid, axis=1, keepdims=True)
    high = square.astype(BF16).astype(F32)
    mid = (square - high).astype(BF16).astype(F32)
    low = square - high - mid
    lane128 = iota((ROWS, 128), 1)
    tail = jnp.where(lane128 == 0, high, jnp.where(lane128 == 1, mid, jnp.where(lane128 == 2, low, 0.0)))
    xbuf[me, :, :SPLIT] = (hid * gain[:, mine]).astype(BF16)
    xbuf[me, :, SPLIT:] = tail.astype(BF16)
    hidden[...] = hid.reshape(2, HALF, SPLIT)
    acc_g[...] = jnp.zeros_like(acc_g)
    acc_u[...] = jnp.zeros_like(acc_u)

    @pl.loop(8, 16)
    def _(i):
        down_load(i).start(priority=1)

    def gate_step(s):
        for copy in gate_load(s):
            copy.wait()
        x = xbuf[step_block(s), :, :SPLIT]
        acc_g[...] += jnp.dot(x, gbuf[s], preferred_element_type=F32)
        acc_u[...] += jnp.dot(x, ubuf[s], preferred_element_type=F32)

    gather(xbuf, x_send, x_recv, gate_step)

    hid_copy = remote(hidden.at[1 - c], hid_own.at[c], hid_sem.at[0], hid_sem.at[1], core_id)
    hid_copy.start()
    hid_own[c] = hidden[c]

    square = jnp.sum(jnp.sum(xbuf[:, :, SPLIT:].astype(F32), axis=0), axis=1, keepdims=True)
    scale = lax.rsqrt(square / D + EPSILON)
    gate = acc_g[...] * scale
    up = acc_u[...] * scale
    act[...] = (gate / (1.0 + jnp.exp(-gate)) * up).astype(BF16)

    def s1_copy(q):
        return remote(s1_send.at[q], s1_recv.at[q], s1_ssem.at[q], s1_rsem.at[q], core_id)

    def s2_copy(u):
        return remote(s2_send.at[u], s2_recv.at[u], s2_ssem.at[u], s2_rsem.at[u], y_id)

    def s3_copy(u):
        return remote(s3_send.at[u], s3_recv.at[u], s3_ssem.at[u], s3_rsem.at[u], z_id(1 + u))

    def down_step(q):
        for half in range(2):
            down_load(2 * q + half).wait()
            piece = jnp.dot(act[...], pool[(2 * q + half + 8) % 16], preferred_element_type=F32)
            part[q, :, :, half * SPLIT : (half + 1) * SPLIT] = piece.reshape(2, HALF, SPLIT)
        s1_send[q] = part[q, 1 - c].astype(BF16)
        s1_copy(q).start()

    def chip_sum(q):
        s1_copy(q).wait_recv()
        return part[q, c] + s1_recv[q].astype(F32)

    def pass_y(u):
        s2_send[u] = chip_sum(u).astype(BF16)
        s2_copy(u).start()

    def pair_sum(u):
        total = chip_sum(ZN + u)
        s2_copy(u).wait_recv()
        return total + s2_recv[u].astype(F32)

    down_step(0)

    @pl.loop(1, ZN)
    def _(q):
        down_step(q)
        pass_y(q - 1)

    down_step(ZN)
    pass_y(ZN - 1)

    @pl.loop(0, ZN - 1)
    def _(u):
        down_step(ZN + 1 + u)
        s3_send[u] = pair_sum(u).astype(BF16)
        s3_copy(u).start()

    total = pair_sum(ZN - 1)
    for u in range(ZN - 1):
        s3_copy(u).wait_recv()
        total = total + s3_recv[u].astype(F32)
    kept = jnp.zeros((HALF, 128), jnp.int32)
    sub16 = iota((HALF, 128), 0)
    for i in range(HALF):
        kept = jnp.where(sub16 == i, kept_rows[i], kept)
    kept = kept.astype(F32)[:, :1]
    hid_copy.wait()
    for half in range(2):
        cols = slice(half * SPLIT, (half + 1) * SPLIT)
        out[:, cols] = (hid_own[half] + kept * total[:, cols]).astype(BF16)

    gather_end(ctx, ctx_send, ctx_recv)
    gather_end(xbuf, x_send, x_recv)
    for q in range(8):
        s1_copy(q).wait_send()
    for u in range(ZN):
        s2_copy(u).wait_send()
    for u in range(ZN - 1):
        s3_copy(u).wait_send()


def fused_device(
    queries, key_cache, value_cache, lengths, slot_order, kept_rows, residual, norm_gain, w_out, w_gate, w_up, w_down
):
    vmem = pl.BlockSpec(memory_space=pltpu.VMEM)
    smem = pl.BlockSpec(memory_space=pltpu.SMEM)
    hbm = pl.BlockSpec(memory_space=pl.ANY)
    slots = key_cache.shape[1]
    dma = pltpu.SemaphoreType.DMA
    return pl.pallas_call(
        fused_kernel,
        out_shape=jax.ShapeDtypeStruct((HALF, 1024), BF16),
        in_specs=[vmem, hbm, hbm, smem, smem, smem, vmem, vmem, hbm, hbm, hbm, hbm],
        out_specs=vmem,
        scratch_shapes=[
            pltpu.VMEM((2, slots, 1024), BF16),
            pltpu.VMEM((2, slots, 1024), BF16),
            pltpu.VMEM((2, 64, 1024), F32),
            pltpu.VMEM((NDEV, 16, 1024), BF16),
            pltpu.VMEM((KVH, ROWS, 256), BF16),
            pltpu.VMEM((KVH, ROWS, 1024), BF16),
            pltpu.VMEM((16, 1024, SPLIT), BF16),
            pltpu.VMEM((NDEV, SPLIT, 1024), BF16),
            pltpu.VMEM((NDEV, SPLIT, 1024), BF16),
            pltpu.VMEM((NDEV, ROWS, SPLIT + 128), BF16),
            pltpu.VMEM((ROWS, 1024), F32),
            pltpu.VMEM((ROWS, 1024), F32),
            pltpu.VMEM((2, HALF, SPLIT), F32),
            pltpu.VMEM((2, HALF, SPLIT), F32),
            pltpu.VMEM((ROWS, 1024), BF16),
            pltpu.VMEM((8, 2, HALF, 1024), F32),
            pltpu.VMEM((8, HALF, 1024), BF16),
            pltpu.VMEM((8, HALF, 1024), BF16),
            pltpu.VMEM((4, HALF, 1024), BF16),
            pltpu.VMEM((4, HALF, 1024), BF16),
            pltpu.VMEM((3, HALF, 1024), BF16),
            pltpu.VMEM((3, HALF, 1024), BF16),
            dma((2, 2)), dma((8,)), dma((16,)), dma((16,)), dma((16,)),
            dma((15,)), dma((NDEV,)), dma((15,)), dma((NDEV,)), dma((2,)),
            dma((8,)), dma((8,)), dma((4,)), dma((4,)), dma((3,)), dma((3,)),
        ],
        compiler_params=pltpu.CompilerParams(
            collective_id=0, has_side_effects=True, vmem_limit_bytes=60 * 1024 * 1024
        ),
        cost_estimate=pl.CostEstimate(flops=2 * 32 * 29 * 1024 * 1024, bytes_accessed=60 * 1024 * 1024, transcendentals=0),
        name="decode_step",
    )(
        queries, key_cache, value_cache, lengths, slot_order, kept_rows, residual,
        norm_gain.reshape(1, -1), w_out, w_gate, w_up, w_down,
    )


def solution(mesh):
    return jax.shard_map(
        fused_device if mesh.shape["attn"] == 8 and mesh.shape["ffn"] == 2 else per_device,
        mesh=mesh,
        in_specs=(
            P(("grp", "attn", "ffn"), None),
            P(("grp", "attn", "ffn"), None, None),
            P(("grp", "attn", "ffn"), None, None),
            P(("grp", "attn", "ffn")),
            P("grp"),
            P(("grp", "ffn")),
            P("grp", "attn"),
            P("attn"),
            P(None, "attn"),
            P(None, ("attn", "ffn")),
            P(None, ("attn", "ffn")),
            P(("attn", "ffn"), None),
        ),
        out_specs=P(("grp", "ffn"), "attn"),
        check_vma=False,
    )
```
